256 devices in a mesh: dp: 32 (over y, z), tensor: 8 (over x, core).
Axes of the slice: x: 4, y: 4, z: 8, core: 2. Of those that a mesh axis runs over, the one named last changes fastest.
Arguments:
- activations: bfloat16 [65536, 5120], P('dp'), may hold values from -20 to 20, as said below
- out_grads: bfloat16 [65536, 2560], P('dp', 'tensor'), may hold values from -0.3125 to 0.3125, as said below
- error_memory: bfloat16 [32, 2560, 5120], P('dp', 'tensor'), may hold values from -6 to 6
- warm_start: bfloat16 [2560, 64], P('tensor'), may hold values from -6 to 6
Outputs:
- update: bfloat16 [2560, 5120], P('tensor')
- new_error: bfloat16 [32, 2560, 5120], P('dp', 'tensor')
- next_start: float32 [2560, 64], P('tensor')
The draws below stay inside these ranges and needn't reach their ends.
Inputs may be any that keep to these rules, and one draw needn't show every extreme that they name: activations of each replica share a common part and have feature scales that differ. `out_grads`: cotangents of each replica share a common part.
All inputs are finite; a program needn't handle non-finite values.
Results may differ from the reference program's by a relative error of at most 0.007.
Values may be sent and summed in bfloat16 or wider, within the bound.
No kernel may reach another device: no remote copies, remote signals or barrier semaphores. Data moves between devices by JAX's collectives and lax.ppermute only.
A program may use at most 128 MiB of HBM per device.

```python
import math
import jax
import jax.numpy as jnp
from jax import lax

D = 5120
C = 2560
R = 64
TOK_DEV = 2048
TOKENS = 65536
REPLICAS = 32
N_DP = 32


def draw_activations(key, part):
    key = jax.random.fold_in(key, 11)
    key_shared, key_own, key_cols = jax.random.split(key, 3)
    shared = jax.random.normal(key_shared, (TOK_DEV, D), jnp.float32)
    own = jax.random.normal(key_own, (TOKENS, D), jnp.float32)
    scales = jnp.exp(jax.random.uniform(key_cols, (D,), jnp.float32, math.log(0.3), math.log(3.0)))
    values = (jnp.tile(shared, (TOKENS // TOK_DEV, 1)) + own) * scales * 0.7
    return jnp.clip(values, -20.0, 20.0).astype(jnp.bfloat16)


def draw_out_grads(key, part):
    key = jax.random.fold_in(key, 23)
    key_shared, key_own, key_cols = jax.random.split(key, 3)
    shared = jax.random.normal(key_shared, (TOK_DEV, C), jnp.float32)
    own = jax.random.normal(key_own, (TOKENS, C), jnp.float32)
    scales = jnp.exp(jax.random.uniform(key_cols, (C,), jnp.float32, math.log(0.5), math.log(2.0)))
    factor_scale = (2.0 * TOK_DEV) ** (-0.5)
    values = (jnp.tile(shared, (TOKENS // TOK_DEV, 1)) + own) * scales * factor_scale
    return jnp.clip(values, -20.0 * factor_scale, 20.0 * factor_scale).astype(jnp.bfloat16)


def level_of(rng, dims, cuts, low, largest):
    def one(dim, parts):
        heights = jax.random.uniform(jax.random.fold_in(jax.random.fold_in(rng, 6), dim), (parts,), jnp.float32, low / len(cuts), largest / len(cuts))
        return jnp.repeat(jnp.exp(heights), dims[dim] // parts).reshape((-1,) + (1,) * (len(dims) - dim - 1))

    gain = one(*cuts[0])
    for cut in cuts[1:]:
        gain = gain * one(*cut)
    return gain


def gaussian(own_key, dims, width, most, cuts=(), dtype=jnp.bfloat16):
    factor_of = level_of(own_key, dims, cuts, -0.22, 0.18) if cuts else 1.0
    drawn = jax.random.normal(own_key, dims, jnp.float32) * width * factor_of
    return jnp.minimum(jnp.maximum(drawn, -most), most).astype(dtype)


def setup_inputs(seed: int = 0) -> dict:
    keys = jax.random.split(jax.random.key(seed), 5)
    return {
        "activations": draw_activations(jax.random.fold_in(keys[4], 71), 0),
        "out_grads": draw_out_grads(jax.random.fold_in(keys[4], 71), 0),
        "error_memory": gaussian(keys[2], (REPLICAS, C, D), 1.0, 6.0, ((0, 32), (1, 8))),
        "warm_start": gaussian(keys[3], (C, R), 1.0, 6.0, ((0, 8),)),
    }


CONTRACT_ROWS = (((0,), (0,)), ((), ()))

def merged_block(operands):
    tokens_block, grads_block, memory_block = operands
    gradient = lax.dot_general(grads_block.astype(jnp.float32), tokens_block.astype(jnp.float32), CONTRACT_ROWS, preferred_element_type=jnp.float32)
    return (gradient + memory_block.astype(jnp.float32)).astype(jnp.bfloat16)

def reference(activations, out_grads, error_memory, warm_start):
    tokens_all = activations.reshape(N_DP, TOK_DEV, D)
    grads_all = out_grads.reshape(N_DP, TOK_DEV, C)
    merged = lax.map(merged_block, (tokens_all, grads_all, error_memory))

    def add_sketch(running, matrix):
        term = lax.dot_general(matrix.astype(jnp.float32), warm_start.astype(jnp.float32), CONTRACT_ROWS, preferred_element_type=jnp.float32)
        return (running + term, None)
    sketch, _ = lax.scan(add_sketch, jnp.zeros((D, R), jnp.float32), merged)
    gram_total = jnp.dot(sketch.T, sketch, precision=lax.Precision.HIGHEST)
    factor = jnp.linalg.cholesky(gram_total)
    ortho_basis = jax.scipy.linalg.solve_triangular(factor, sketch.T, lower=True).T
    basis_half = ortho_basis.astype(jnp.bfloat16)

    def add_coeff(running, matrix):
        return (running + jnp.dot(matrix.astype(jnp.float32), basis_half.astype(jnp.float32), preferred_element_type=jnp.float32), None)
    coeff_sum, _ = lax.scan(add_coeff, jnp.zeros((C, R), jnp.float32), merged)
    next_start = coeff_sum / N_DP
    start_half = next_start.astype(jnp.bfloat16)
    decoded = lax.dot_general(start_half.astype(jnp.float32), basis_half.astype(jnp.float32), (((1,), (1,)), ((), ())), preferred_element_type=jnp.float32)
    update = decoded.astype(jnp.bfloat16)

    def residual_block(matrix):
        return (matrix.astype(jnp.float32) - decoded).astype(jnp.bfloat16)
    new_error = lax.map(residual_block, merged)
    return (update, new_error, next_start)
```

```python
import jax
import jax.numpy as jnp
from jax import lax
from jax.experimental import pallas as pl
from jax.experimental.pallas import tpu as pltpu
from jax.sharding import Mesh, PartitionSpec as P

D = 5120
C = 320
R = 64
TOK = 2048
N_DP = 32
N_X, N_Y, N_Z = 4, 4, 8
HALF = D // 2
BLK = 512
MXU = 256
PIECE = 512
PIECES = TOK // PIECE
SLOTS = 3
LANES = 128
GROUP = N_X * LANES
STEPS = D // BLK
HSTEPS = STEPS // 2
ROWS = R // N_Y
COLS = HALF // N_X
PARTS = N_X * N_Y
PAD = 384
F32, BF16 = jnp.float32, jnp.bfloat16
NT = (((1,), (1,)), ((), ()))
TN = (((0,), (0,)), ((), ()))
MIB = 1024 * 1024


def merge_body(
    core_ref, grads_hbm, tokens_hbm, memory_hbm, warm_hbm, merged_ref, send_ref, own_ref,
    grads, tokens, memory, low_rows, warm, warm_copied, grads_sem, tokens_sem, memory_sem, warm_sem,
):
    core = core_ref[0]

    def column(j):
        half = jnp.where(j < HSTEPS, 1 - core, core)
        return pl.multiple_of((half * HSTEPS + lax.rem(j, HSTEPS)) * BLK, BLK)

    def grads_copy(i):
        at = pl.ds(i * PIECE, PIECE)
        return pltpu.make_async_copy(grads_hbm.at[:, at], grads.at[:, at], grads_sem.at[i])

    def tokens_copy(j, i):
        slot, at = lax.rem(j, SLOTS), pl.ds(i * PIECE, PIECE)
        return pltpu.make_async_copy(
            tokens_hbm.at[at, pl.ds(column(j), BLK)], tokens.at[slot, at], tokens_sem.at[slot, i]
        )

    def memory_copy(j):
        slot = lax.rem(j, SLOTS)
        return pltpu.make_async_copy(
            memory_hbm.at[:, pl.ds(column(j), BLK)], memory.at[slot], memory_sem.at[slot]
        )

    def fetch(j):
        for i in range(PIECES):
            tokens_copy(j, i).start()
        memory_copy(j).start()

    first = jnp.int32(0)
    for i in range(PIECES):
        grads_copy(i).start()
        tokens_copy(first, i).start()
    memory_copy(first).start()
    for j in range(1, SLOTS - 1):
        fetch(jnp.int32(j))
    warm_copy = pltpu.make_async_copy(warm_hbm, warm_copied, warm_sem)
    warm_copy.start()
    low_rows[...] = jnp.zeros_like(low_rows)
    warm[...] = jnp.zeros_like(warm)

    def on_accumulators(acc0, acc1, part0, part1):
        accs, sums = (acc0, acc1), (part0, part1)

        def multiply(j, begin):
            slot = lax.rem(j, SLOTS)
            for i in range(PIECES):
                if begin:
                    grads_copy(i).wait()
                tokens_copy(j, i).wait()
                for k in range(i * PIECE // MXU, (i + 1) * PIECE // MXU):
                    depth = slice(k * MXU, (k + 1) * MXU)
                    for h in range(2):
                        pltpu.matmul_push_rhs(tokens[slot, depth, h * MXU : (h + 1) * MXU], k % 2, h)
                    left = grads[:, depth]
                    for acc in accs:
                        pltpu.matmul_acc_lhs(acc, left, k % 2)

        def finish(j):
            slot = lax.rem(j, SLOTS)
            memory_copy(j).wait()
            for h, acc in enumerate(accs):
                gradient = pltpu.matmul_pop(acc)
                merged = (gradient + memory[slot, :, h * MXU : (h + 1) * MXU].astype(F32)).astype(BF16)
                merged_ref[:, pl.ds(column(j) + h * MXU, MXU)] = merged
                low_rows[h, 0 : C - MXU, :] = merged[MXU:]

        def sketch_start(j):
            for h, part in enumerate(sums):
                pltpu.matmul_push_rhs(merged_ref[0:MXU, pl.ds(column(j) + h * MXU, MXU)], 0, h)
                pltpu.matmul_push_rhs(low_rows[h], 1, h)
                pltpu.matmul_acc_lhs(part, warm[:, 0:MXU], 0)
                pltpu.matmul_acc_lhs(part, warm[:, MXU:], 1)

        def sketch_end(j):
            at = pl.ds(pl.multiple_of(lax.rem(j, HSTEPS) * LANES, LANES), LANES)
            terms = [pltpu.matmul_pop(part) for part in sums]

            def put(ref):
                for q in range(N_X):
                    term = terms[q // 2][:, q % 2 * LANES : (q % 2 + 1) * LANES].astype(ref.dtype)
                    for p in range(N_Y):
                        ref[q * N_Y + p, :, at] = term[p * ROWS : (p + 1) * ROWS]

            @pl.when(j < HSTEPS)
            def _():
                put(send_ref)

            @pl.when(j >= HSTEPS)
            def _():
                put(own_ref)

        def advance(j):
            @pl.when(j + SLOTS - 1 < STEPS)
            def _():
                fetch(j + SLOTS - 1)

        advance(first)
        multiply(first, True)
        warm_copy.wait()
        warm[:, 0:C] = warm_copied[...]
        finish(first)

        def step(j, carry):
            advance(j)
            multiply(j, False)
            sketch_start(j - 1)
            finish(j)
            sketch_end(j - 1)
            return carry

        lax.fori_loop(1, STEPS, step, 0)
        last = jnp.int32(STEPS - 1)
        sketch_start(last)
        sketch_end(last)

    pl.run_scoped(
        on_accumulators,
        pltpu.ACC(0)((C, MXU), F32),
        pltpu.ACC(1)((C, MXU), F32),
        pltpu.ACC(0)((R, MXU), F32),
        pltpu.ACC(1)((R, MXU), F32),
    )


def merge(core, grads_t, tokens, memory, warm_t):
    vmem, hbm = pl.BlockSpec(memory_space=pltpu.VMEM), pl.BlockSpec(memory_space=pltpu.HBM)
    return pl.pallas_call(
        merge_body,
        out_shape=(
            jax.ShapeDtypeStruct((C, D), BF16),
            jax.ShapeDtypeStruct((PARTS, ROWS, COLS), BF16),
            jax.ShapeDtypeStruct((PARTS, ROWS, COLS), F32),
        ),
        in_specs=[pl.BlockSpec(memory_space=pltpu.SMEM), hbm, hbm, hbm, hbm],
        out_specs=(vmem, vmem, vmem),
        scratch_shapes=[
            pltpu.VMEM((C, TOK), BF16),
            pltpu.VMEM((SLOTS, TOK, BLK), BF16),
            pltpu.VMEM((SLOTS, C, BLK), BF16),
            pltpu.VMEM((2, MXU, MXU), BF16),
            pltpu.VMEM((R, 2 * MXU), BF16),
            pltpu.VMEM((R, C), BF16),
            pltpu.SemaphoreType.DMA((PIECES,)),
            pltpu.SemaphoreType.DMA((SLOTS, PIECES)),
            pltpu.SemaphoreType.DMA((SLOTS,)),
            pltpu.SemaphoreType.DMA(()),
        ],
        compiler_params=pltpu.CompilerParams(vmem_limit_bytes=24 * MIB),
        cost_estimate=pl.CostEstimate(flops=2 * C * D * (TOK + R), bytes_accessed=30_000_000, transcendentals=0),
        name="merge",
    )(core, *(pltpu.with_memory_space_constraint(x, pltpu.HBM) for x in (grads_t, tokens, memory, warm_t)))


def coeff_body(core_ref, own_ref, other_ref, merged_ref, coeff_ref, gram_ref, sketch_hbm, sketch_ref, sketch_sem):
    core = core_ref[0]
    for ref, half in ((own_ref, core), (other_ref, 1 - core)):
        for b in range(HALF // GROUP):
            for q in range(N_X):
                at = pl.ds(pl.multiple_of(half * HALF + b * GROUP + q * LANES, LANES), LANES)
                for p in range(N_Y):
                    sketch_ref[p * ROWS : (p + 1) * ROWS, at] = ref[q * N_Y + p, :, b * LANES : (b + 1) * LANES]
    copy = pltpu.make_async_copy(sketch_ref, sketch_hbm, sketch_sem)
    copy.start()
    sketch = sketch_ref[...]
    gram_ref[...] = lax.dot_general(sketch, sketch, NT, preferred_element_type=F32)
    coeff = lax.dot_general(sketch, merged_ref[...], NT, preferred_element_type=F32)
    each = R // N_DP
    for i in range(N_DP):
        coeff_ref[i, :, 0:C] = coeff[i * each : (i + 1) * each]
        coeff_ref[i, :, C:] = jnp.zeros((each, PAD - C), F32)
    copy.wait()


def coefficients(core, own, other, merged):
    vmem = pl.BlockSpec(memory_space=pltpu.VMEM)
    return pl.pallas_call(
        coeff_body,
        out_shape=(
            jax.ShapeDtypeStruct((N_DP, R // N_DP, PAD), F32),
            jax.ShapeDtypeStruct((R, R), F32),
            pltpu.HBM((R, D), BF16),
        ),
        in_specs=[pl.BlockSpec(memory_space=pltpu.SMEM), vmem, vmem, vmem],
        out_specs=(vmem, vmem, pl.BlockSpec(memory_space=pltpu.HBM)),
        scratch_shapes=[pltpu.VMEM((R, D), BF16), pltpu.SemaphoreType.DMA(())],
        compiler_params=pltpu.CompilerParams(vmem_limit_bytes=8 * MIB),
        cost_estimate=pl.CostEstimate(flops=2 * C * D * R, bytes_accessed=5_000_000, transcendentals=0),
        name="coefficients",
    )(core, own, other, merged)


def basis_body(gram_ref, sketch_hbm, inverse_ref, basis_hbm, sketch_ref, basis_ref, sketch_sem, basis_sem):
    sketch_copy = pltpu.make_async_copy(sketch_hbm, sketch_ref, sketch_sem)
    sketch_copy.start()
    row = lax.broadcasted_iota(jnp.int32, (R, R), 0)
    col = lax.broadcasted_iota(jnp.int32, (R, R), 1)
    state = jnp.concatenate([gram_ref[...], (row == col).astype(F32)], axis=1)
    index = lax.broadcasted_iota(jnp.int32, (R, 1), 0)
    for j in range(R - 1):
        top = (j + 1) // 8 * 8
        lead = state[j : j + 1, :]
        ratio = jnp.where(index[top:] > j, state[top:, j : j + 1] / lead[:, j : j + 1], 0.0)
        tail = state[top:, :] - ratio * lead
        state = tail if top == 0 else jnp.concatenate([state[:top], tail], axis=0)
    diagonal = jnp.sum(jnp.where(row == col, state[:, :R], 0.0), axis=1, keepdims=True)
    inverse = state[:, R:] * lax.rsqrt(diagonal)
    inverse_ref[...] = inverse
    high = inverse.astype(BF16)
    rest = inverse - high.astype(F32)
    middle = rest.astype(BF16)
    low = (rest - middle.astype(F32)).astype(BF16)
    sketch_copy.wait()
    sketch = sketch_ref[...]
    out = jnp.dot(high, sketch, preferred_element_type=F32)
    out += jnp.dot(middle, sketch, preferred_element_type=F32)
    out += jnp.dot(low, sketch, preferred_element_type=F32)
    basis_ref[...] = out.astype(BF16)
    basis_copy = pltpu.make_async_copy(basis_ref, basis_hbm, basis_sem)
    basis_copy.start()
    basis_copy.wait()


def basis(gram, sketch_t):
    vmem, hbm = pl.BlockSpec(memory_space=pltpu.VMEM), pl.BlockSpec(memory_space=pltpu.HBM)
    return pl.pallas_call(
        basis_body,
        out_shape=(jax.ShapeDtypeStruct((R, R), F32), pltpu.HBM((R, D), BF16)),
        in_specs=[vmem, hbm],
        out_specs=(vmem, hbm),
        scratch_shapes=[
            pltpu.VMEM((R, D), BF16),
            pltpu.VMEM((R, D), BF16),
            pltpu.SemaphoreType.DMA(()),
            pltpu.SemaphoreType.DMA(()),
        ],
        compiler_params=pltpu.CompilerParams(vmem_limit_bytes=8 * MIB),
        cost_estimate=pl.CostEstimate(flops=2 * R * R * D * 6, bytes_accessed=20_000_000, transcendentals=0),
        name="basis",
    )(gram, pltpu.with_memory_space_constraint(sketch_t, pltpu.HBM))


def decode_body(
    total_ref, inverse_ref, basis_hbm, merged_ref, update_hbm, error_hbm, start_ref,
    basis, update, error, basis_sem, update_sem, error_sem,
):
    blocks = [pl.ds(j * DBLK, DBLK) for j in range(DSTEPS)]
    arrivals = [
        pltpu.make_async_copy(basis_hbm.at[:, at], basis.at[:, at], basis_sem.at[j]) for j, at in enumerate(blocks)
    ]
    for copy in arrivals:
        copy.start()
    total = jnp.concatenate([total_ref[i, :, 0:C] for i in range(N_DP)], axis=0)
    start = jnp.dot(inverse_ref[...], total, precision=lax.Precision.HIGHEST, preferred_element_type=F32) * (1.0 / N_DP)
    start_ref[...] = start
    half = start.astype(BF16).T
    copies = []
    for j, at in enumerate(blocks):
        arrivals[j].wait()
        decoded = jnp.dot(half, basis[:, at], preferred_element_type=F32)
        update[:, at] = decoded.astype(BF16)
        error[:, at] = (merged_ref[:, at].astype(F32) - decoded).astype(BF16)
        copies.append(pltpu.make_async_copy(update.at[:, at], update_hbm.at[:, at], update_sem.at[j]))
        copies.append(pltpu.make_async_copy(error.at[:, at], error_hbm.at[:, at], error_sem.at[j]))
        copies[-2].start()
        copies[-1].start()
    for copy in copies:
        copy.wait()


DBLK = 512
DSTEPS = D // DBLK


def decode(total, inverse, basis_t, merged):
    vmem, hbm = pl.BlockSpec(memory_space=pltpu.VMEM), pl.BlockSpec(memory_space=pltpu.HBM)
    return pl.pallas_call(
        decode_body,
        out_shape=(
            jax.ShapeDtypeStruct((C, D), BF16),
            jax.ShapeDtypeStruct((C, D), BF16),
            jax.ShapeDtypeStruct((R, C), F32),
        ),
        in_specs=[vmem, vmem, hbm, vmem],
        out_specs=(hbm, hbm, vmem),
        scratch_shapes=[
            pltpu.VMEM((R, D), BF16),
            pltpu.VMEM((C, D), BF16),
            pltpu.VMEM((C, D), BF16),
            pltpu.SemaphoreType.DMA((DSTEPS,)),
            pltpu.SemaphoreType.DMA((DSTEPS,)),
            pltpu.SemaphoreType.DMA((DSTEPS,)),
        ],
        compiler_params=pltpu.CompilerParams(vmem_limit_bytes=16 * MIB),
        cost_estimate=pl.CostEstimate(flops=2 * C * D * R, bytes_accessed=10_500_000, transcendentals=0),
        name="decode",
    )(total, inverse, pltpu.with_memory_space_constraint(basis_t, pltpu.HBM), merged)


def add_up_body(parts_ref, out_ref):
    total = jnp.sum(parts_ref[...].astype(F32), axis=0).astype(out_ref.dtype)
    for i in range(out_ref.shape[0]):
        out_ref[i] = total


def add_up(parts, copies):
    vmem = pl.BlockSpec(memory_space=pltpu.VMEM)
    return pl.pallas_call(
        add_up_body,
        out_shape=jax.ShapeDtypeStruct((copies, *parts.shape[1:]), parts.dtype),
        in_specs=[vmem],
        out_specs=vmem,
        compiler_params=pltpu.CompilerParams(vmem_limit_bytes=4 * MIB),
        cost_estimate=pl.CostEstimate(flops=parts.size, bytes_accessed=2 * parts.size, transcendentals=0),
        name="add_up",
    )(parts)


def per_device(activations, out_grads, error_memory, warm_start):
    core = lax.axis_index("core").astype(jnp.int32).reshape(1)
    swap = [(0, 1), (1, 0)]
    merged, send, own = merge(core, out_grads.T, activations, error_memory[0], warm_start.T)
    mine = (own + lax.ppermute(send, "core", swap).astype(F32)).astype(BF16)
    parts = lax.all_to_all(mine, ("y", "x"), 0, 0, tiled=True)
    parts = lax.all_to_all(add_up(parts, N_Z), "z", 0, 0, tiled=True)
    sketch_own = lax.all_to_all(add_up(parts, PARTS), ("y", "x"), 0, 0, tiled=True)
    sketch_other = lax.ppermute(sketch_own, "core", swap)
    coeff, gram, sketch_t = coefficients(core, sketch_own, sketch_other, merged)
    terms = lax.all_to_all(coeff, ("y", "z"), 0, 0, tiled=True)
    total = lax.all_to_all(add_up(terms, N_DP), ("y", "z"), 0, 0, tiled=True)
    inverse, basis_t = basis(gram, sketch_t)
    update, new_error, start_t = decode(total, inverse, basis_t, merged)
    return update, new_error[None], start_t.T


def solution(mesh):
    fine = Mesh(mesh.devices.reshape(N_Y, N_Z, N_X, 2), ("y", "z", "x", "core"))
    d, t = ("y", "z"), ("x", "core")
    return jax.shard_map(
        per_device,
        mesh=fine,
        in_specs=(P(d, None), P(d, t), P(d, t, None), P(t, None)),
        out_specs=(P(t, None), P(d, t, None), P(t, None)),
        check_vma=False,
    )
```

```python
import jax
import jax.numpy as jnp
from jax import lax
from jax.experimental import pallas as pl
from jax.experimental.pallas import tpu as pltpu
from jax.sharding import Mesh, PartitionSpec as P

D = 5120
C = 320
R = 64
TOK = 2048
N_DP = 32
N_X, N_Y, N_Z = 4, 4, 8
HALF = D // 2
BLK = 512
MXU = 256
SLOTS = 3
LANES = 128
GROUP = N_X * LANES
STEPS = D // BLK
KEPT = 6
WIDE = KEPT * BLK
HSTEPS = STEPS // 2
ROWS = R // N_Y
COLS = HALF // N_X
PARTS = N_X * N_Y
PAD = 384
F32, BF16 = jnp.float32, jnp.bfloat16
NT = (((1,), (1,)), ((), ()))
TN = (((0,), (0,)), ((), ()))
MIB = 1024 * 1024


def merge_body(
    core_ref, grads_hbm, tokens_hbm, memory_hbm, warm_hbm, kept_ref, rest_ref, rest_hbm, send_ref, own_ref,
    grads, tokens, memory, high_rows, low_rows, warm, warm_copied, grads_sem, tokens_sem, memory_sem, warm_sem, rest_sem,
):
    core = core_ref[0]

    def block(j):
        half = jnp.where(j < HSTEPS, 1 - core, core)
        return half * HSTEPS + lax.rem(j + half * (KEPT - HSTEPS), HSTEPS)

    def column(j):
        return pl.multiple_of(block(j) * BLK, BLK)

    def spill(j):
        at = pl.ds(pl.multiple_of((block(j) - KEPT) * BLK, BLK), BLK)
        return pltpu.make_async_copy(rest_ref.at[:, at], rest_hbm.at[:, at], rest_sem.at[block(j) - KEPT])

    grads_copy = pltpu.make_async_copy(grads_hbm, grads, grads_sem)

    def copies(j):
        slot, at = lax.rem(j, SLOTS), pl.ds(column(j), BLK)
        return (
            pltpu.make_async_copy(tokens_hbm.at[:, at], tokens.at[slot], tokens_sem.at[slot]),
            pltpu.make_async_copy(memory_hbm.at[:, at], memory.at[slot], memory_sem.at[slot]),
        )

    def fetch(j):
        for copy in copies(j):
            copy.start()

    def arrive(j):
        for copy in copies(j):
            copy.wait()

    first = jnp.int32(0)
    grads_copy.start()
    fetch(first)
    warm_copy = pltpu.make_async_copy(warm_hbm, warm_copied, warm_sem)
    warm_copy.start()
    low_rows[...] = jnp.zeros_like(low_rows)
    warm[...] = jnp.zeros_like(warm)

    def on_accumulators(acc0, acc1, part0, part1):
        accs, sums = (acc0, acc1), (part0, part1)

        def multiply(j):
            slot = lax.rem(j, SLOTS)
            for k in range(TOK // MXU):
                depth = slice(k * MXU, (k + 1) * MXU)
                for h in range(2):
                    pltpu.matmul_push_rhs(tokens[slot, depth, h * MXU : (h + 1) * MXU], k % 2, h)
                left = grads[:, depth]
                for acc in accs:
                    pltpu.matmul_acc_lhs(acc, left, k % 2)

        def finish(j):
            slot = lax.rem(j, SLOTS)
            for h, acc in enumerate(accs):
                gradient = pltpu.matmul_pop(acc)
                merged = (gradient + memory[slot, :, h * MXU : (h + 1) * MXU].astype(F32)).astype(BF16)
                high_rows[h] = merged[0:MXU]
                low_rows[h, 0 : C - MXU, :] = merged[MXU:]

                @pl.when(block(j) < KEPT)
                def _():
                    kept_ref[:, pl.ds(column(j) + h * MXU, MXU)] = merged

                @pl.when(block(j) >= KEPT)
                def _():
                    rest_ref[:, pl.ds(column(j) - WIDE + h * MXU, MXU)] = merged

            @pl.when(block(j) >= KEPT)
            def _():
                spill(j).start()

        def sketch_start(j):
            for h, part in enumerate(sums):
                pltpu.matmul_push_rhs(high_rows[h], 0, h)
                pltpu.matmul_push_rhs(low_rows[h], 1, h)
                pltpu.matmul_acc_lhs(part, warm[:, 0:MXU], 0)
                pltpu.matmul_acc_lhs(part, warm[:, MXU:], 1)

        def sketch_end(j):
            at = pl.ds(pl.multiple_of(lax.rem(block(j), HSTEPS) * LANES, LANES), LANES)
            terms = [pltpu.matmul_pop(part) for part in sums]

            def put(ref):
                for q in range(N_X):
                    term = terms[q // 2][:, q % 2 * LANES : (q % 2 + 1) * LANES].astype(ref.dtype)
                    for p in range(N_Y):
                        ref[q * N_Y + p, :, at] = term[p * ROWS : (p + 1) * ROWS]

            @pl.when(j < HSTEPS)
            def _():
                put(send_ref)

            @pl.when(j >= HSTEPS)
            def _():
                put(own_ref)

        grads_copy.wait()
        fetch(first + 1)
        arrive(first)
        for j in range(2, SLOTS):
            fetch(jnp.int32(j))
        multiply(first)
        warm_copy.wait()
        warm[:, 0:C] = warm_copied[...]
        finish(first)

        def step(j, carry):
            arrive(j)

            @pl.when(j + SLOTS - 1 < STEPS)
            def _():
                fetch(j + SLOTS - 1)

            multiply(j)
            sketch_start(j - 1)
            finish(j)
            sketch_end(j - 1)
            return carry

        lax.fori_loop(1, STEPS, step, 0)
        last = jnp.int32(STEPS - 1)
        sketch_start(last)
        sketch_end(last)
        for i in range(STEPS - KEPT):
            at = pl.ds(i * BLK, BLK)
            pltpu.make_async_copy(rest_ref.at[:, at], rest_hbm.at[:, at], rest_sem.at[i]).wait()

    pl.run_scoped(
        on_accumulators,
        pltpu.ACC(0)((C, MXU), F32),
        pltpu.ACC(1)((C, MXU), F32),
        pltpu.ACC(0)((R, MXU), F32),
        pltpu.ACC(1)((R, MXU), F32),
    )


def merge(core, grads_t, tokens, memory, warm_t):
    vmem, hbm = pl.BlockSpec(memory_space=pltpu.VMEM), pl.BlockSpec(memory_space=pltpu.HBM)
    return pl.pallas_call(
        merge_body,
        out_shape=(
            jax.ShapeDtypeStruct((C, WIDE), BF16),
            jax.ShapeDtypeStruct((C, D - WIDE), BF16),
            pltpu.HBM((C, D - WIDE), BF16),
            jax.ShapeDtypeStruct((PARTS, ROWS, COLS), BF16),
            jax.ShapeDtypeStruct((PARTS, ROWS, COLS), F32),
        ),
        in_specs=[pl.BlockSpec(memory_space=pltpu.SMEM), hbm, hbm, hbm, hbm],
        out_specs=(vmem, vmem, hbm, vmem, vmem),
        scratch_shapes=[
            pltpu.VMEM((C, TOK), BF16),
            pltpu.VMEM((SLOTS, TOK, BLK), BF16),
            pltpu.VMEM((SLOTS, C, BLK), BF16),
            pltpu.VMEM((2, MXU, MXU), BF16),
            pltpu.VMEM((2, MXU, MXU), BF16),
            pltpu.VMEM((R, 2 * MXU), BF16),
            pltpu.VMEM((R, C), BF16),
            pltpu.SemaphoreType.DMA(()),
            pltpu.SemaphoreType.DMA((SLOTS,)),
            pltpu.SemaphoreType.DMA((SLOTS,)),
            pltpu.SemaphoreType.DMA(()),
            pltpu.SemaphoreType.DMA((STEPS - KEPT,)),
        ],
        compiler_params=pltpu.CompilerParams(vmem_limit_bytes=24 * MIB),
        cost_estimate=pl.CostEstimate(flops=2 * C * D * (TOK + R), bytes_accessed=30_000_000, transcendentals=0),
        name="merge",
    )(core, *(pltpu.with_memory_space_constraint(x, pltpu.HBM) for x in (grads_t, tokens, memory, warm_t)))


def coeff_body(core_ref, own_ref, other_ref, kept_ref, rest_ref, coeff_ref, gram_ref, sketch_ref):
    core = core_ref[0]
    for ref, half in ((own_ref, core), (other_ref, 1 - core)):
        for b in range(HALF // GROUP):
            for q in range(N_X):
                at = pl.ds(pl.multiple_of(half * HALF + b * GROUP + q * LANES, LANES), LANES)
                for p in range(N_Y):
                    sketch_ref[p * ROWS : (p + 1) * ROWS, at] = ref[q * N_Y + p, :, b * LANES : (b + 1) * LANES]
    sketch = sketch_ref[...]
    gram_ref[...] = lax.dot_general(sketch, sketch, NT, preferred_element_type=F32)
    coeff = lax.dot_general(sketch[:, :WIDE], kept_ref[...], NT, preferred_element_type=F32)
    coeff += lax.dot_general(sketch[:, WIDE:], rest_ref[...], NT, preferred_element_type=F32)
    each = R // N_DP
    for i in range(N_DP):
        coeff_ref[i, :, 0:C] = coeff[i * each : (i + 1) * each]
        coeff_ref[i, :, C:] = jnp.zeros((each, PAD - C), F32)


def coefficients(core, own, other, kept, rest):
    vmem = pl.BlockSpec(memory_space=pltpu.VMEM)
    return pl.pallas_call(
        coeff_body,
        out_shape=(
            jax.ShapeDtypeStruct((N_DP, R // N_DP, PAD), F32),
            jax.ShapeDtypeStruct((R, R), F32),
            jax.ShapeDtypeStruct((R, D), BF16),
        ),
        in_specs=[pl.BlockSpec(memory_space=pltpu.SMEM), vmem, vmem, vmem, vmem],
        out_specs=(vmem, vmem, vmem),
        compiler_params=pltpu.CompilerParams(vmem_limit_bytes=8 * MIB),
        cost_estimate=pl.CostEstimate(flops=2 * C * D * R, bytes_accessed=5_000_000, transcendentals=0),
        name="coefficients",
    )(core, own, other, kept, rest)


def basis_body(gram_ref, sketch_ref, inverse_ref, basis_ref):
    row = lax.broadcasted_iota(jnp.int32, (R, R), 0)
    col = lax.broadcasted_iota(jnp.int32, (R, R), 1)
    state = jnp.concatenate([gram_ref[...], (row == col).astype(F32)], axis=1)
    index = lax.broadcasted_iota(jnp.int32, (R, 1), 0)
    for j in range(R - 1):
        top = (j + 1) // 8 * 8
        lead = state[j : j + 1, :]
        ratio = jnp.where(index[top:] > j, state[top:, j : j + 1] / lead[:, j : j + 1], 0.0)
        tail = state[top:, :] - ratio * lead
        state = tail if top == 0 else jnp.concatenate([state[:top], tail], axis=0)
    diagonal = jnp.sum(jnp.where(row == col, state[:, :R], 0.0), axis=1, keepdims=True)
    inverse = state[:, R:] * lax.rsqrt(diagonal)
    inverse_ref[...] = inverse
    high = inverse.astype(BF16)
    rest = inverse - high.astype(F32)
    middle = rest.astype(BF16)
    low = (rest - middle.astype(F32)).astype(BF16)
    sketch = sketch_ref[...]
    out = jnp.dot(high, sketch, preferred_element_type=F32)
    out += jnp.dot(middle, sketch, preferred_element_type=F32)
    out += jnp.dot(low, sketch, preferred_element_type=F32)
    basis_ref[...] = out.astype(BF16)


def basis(gram, sketch_t):
    vmem = pl.BlockSpec(memory_space=pltpu.VMEM)
    return pl.pallas_call(
        basis_body,
        out_shape=(jax.ShapeDtypeStruct((R, R), F32), jax.ShapeDtypeStruct((R, D), BF16)),
        in_specs=[vmem, vmem],
        out_specs=(vmem, vmem),
        compiler_params=pltpu.CompilerParams(vmem_limit_bytes=8 * MIB),
        cost_estimate=pl.CostEstimate(flops=2 * R * R * D * 6, bytes_accessed=20_000_000, transcendentals=0),
        name="basis",
    )(gram, sketch_t)


def decode_body(
    total_ref, inverse_ref, basis_ref, kept_ref, rest_hbm, update_hbm, error_hbm, start_ref,
    rest, update, error, rest_sem, update_sem, error_sem,
):
    rest_copy = pltpu.make_async_copy(rest_hbm, rest, rest_sem)
    rest_copy.start()
    total = jnp.concatenate([total_ref[i, :, 0:C] for i in range(N_DP)], axis=0)
    start = jnp.dot(inverse_ref[...], total, precision=lax.Precision.HIGHEST, preferred_element_type=F32) * (1.0 / N_DP)
    start_ref[...] = start
    half = start.astype(BF16).T
    copies = []
    for j in range(DSTEPS):
        at = pl.ds(j * DBLK, DBLK)
        if j * DBLK == WIDE:
            rest_copy.wait()
        merged = kept_ref[:, at] if j * DBLK < WIDE else rest[:, j * DBLK - WIDE : (j + 1) * DBLK - WIDE]
        decoded = jnp.dot(half, basis_ref[:, at], preferred_element_type=F32)
        update[:, at] = decoded.astype(BF16)
        error[:, at] = (merged.astype(F32) - decoded).astype(BF16)
        copies.append(pltpu.make_async_copy(update.at[:, at], update_hbm.at[:, at], update_sem.at[j]))
        copies.append(pltpu.make_async_copy(error.at[:, at], error_hbm.at[:, at], error_sem.at[j]))
        copies[-2].start()
        copies[-1].start()
    for copy in copies:
        copy.wait()


DBLK = 1024
DSTEPS = D // DBLK


def decode(total, inverse, basis_t, kept, rest):
    vmem, hbm = pl.BlockSpec(memory_space=pltpu.VMEM), pl.BlockSpec(memory_space=pltpu.HBM)
    return pl.pallas_call(
        decode_body,
        out_shape=(
            jax.ShapeDtypeStruct((C, D), BF16),
            jax.ShapeDtypeStruct((C, D), BF16),
            jax.ShapeDtypeStruct((R, C), F32),
        ),
        in_specs=[vmem, vmem, vmem, vmem, hbm],
        out_specs=(hbm, hbm, vmem),
        scratch_shapes=[
            pltpu.VMEM((C, D - WIDE), BF16),
            pltpu.VMEM((C, D), BF16),
            pltpu.VMEM((C, D), BF16),
            pltpu.SemaphoreType.DMA(()),
            pltpu.SemaphoreType.DMA((DSTEPS,)),
            pltpu.SemaphoreType.DMA((DSTEPS,)),
        ],
        compiler_params=pltpu.CompilerParams(vmem_limit_bytes=16 * MIB),
        cost_estimate=pl.CostEstimate(flops=2 * C * D * R, bytes_accessed=10_500_000, transcendentals=0),
        name="decode",
    )(total, inverse, basis_t, kept, pltpu.with_memory_space_constraint(rest, pltpu.HBM))


def add_up_body(parts_ref, out_ref):
    total = jnp.sum(parts_ref[...].astype(F32), axis=0).astype(out_ref.dtype)
    for i in range(out_ref.shape[0]):
        out_ref[i] = total


def add_up(parts, copies):
    vmem = pl.BlockSpec(memory_space=pltpu.VMEM)
    return pl.pallas_call(
        add_up_body,
        out_shape=jax.ShapeDtypeStruct((copies, *parts.shape[1:]), parts.dtype),
        in_specs=[vmem],
        out_specs=vmem,
        compiler_params=pltpu.CompilerParams(vmem_limit_bytes=4 * MIB),
        cost_estimate=pl.CostEstimate(flops=parts.size, bytes_accessed=2 * parts.size, transcendentals=0),
        name="add_up",
    )(parts)


def per_device(activations, out_grads, error_memory, warm_start):
    core = lax.axis_index("core").astype(jnp.int32).reshape(1)
    swap = [(0, 1), (1, 0)]
    kept, rest, rest_hbm, send, own = merge(core, out_grads.T, activations, error_memory[0], warm_start.T)
    mine = (own + lax.ppermute(send, "core", swap).astype(F32)).astype(BF16)
    parts = lax.all_to_all(mine, ("y", "x"), 0, 0, tiled=True)
    parts = lax.all_to_all(add_up(parts, N_Z), "z", 0, 0, tiled=True)
    sketch_own = lax.all_to_all(add_up(parts, PARTS), ("y", "x"), 0, 0, tiled=True)
    sketch_other = lax.ppermute(sketch_own, "core", swap)
    coeff, gram, sketch_t = coefficients(core, sketch_own, sketch_other, kept, rest)
    terms = lax.all_to_all(coeff, ("y", "z"), 0, 0, tiled=True)
    total = lax.all_to_all(add_up(terms, N_DP), ("y", "z"), 0, 0, tiled=True)
    inverse, basis_t = basis(gram, sketch_t)
    update, new_error, start_t = decode(total, inverse, basis_t, kept, rest_hbm)
    return update, new_error[None], start_t.T


def solution(mesh):
    fine = Mesh(mesh.devices.reshape(N_Y, N_Z, N_X, 2), ("y", "z", "x", "core"))
    d, t = ("y", "z"), ("x", "core")
    return jax.shard_map(
        per_device,
        mesh=fine,
        in_specs=(P(d, None), P(d, t), P(d, t, None), P(t, None)),
        out_specs=(P(t, None), P(d, t, None), P(t, None)),
        check_vma=False,
    )
```

```python
import jax
import jax.numpy as jnp
from jax import lax
from jax.experimental import pallas as pl
from jax.experimental.pallas import tpu as pltpu
from jax.sharding import Mesh, PartitionSpec as P

D = 5120
C = 320
R = 64
TOK = 2048
N_DP = 32
N_X, N_Y, N_Z = 4, 4, 8
HALF = D // 2
BLK = 512
MXU = 256
SLOTS = 3
LANES = 128
GROUP = N_X * LANES
STEPS = D // BLK
KEPT = 6
WIDE = KEPT * BLK
HSTEPS = STEPS // 2
ROWS = R // N_Y
COLS = HALF // N_X
PARTS = N_X * N_Y
PAD = 384
F32, BF16 = jnp.float32, jnp.bfloat16
NT = (((1,), (1,)), ((), ()))
TN = (((0,), (0,)), ((), ()))
MIB = 1024 * 1024


def merge_body(
    core_ref, grads_hbm, tokens_hbm, memory_hbm, warm_hbm, kept_ref, rest_ref, rest_hbm, send_ref, own_ref,
    grads, tokens, memory, high_rows, low_rows, warm, warm_copied, grads_sem, tokens_sem, memory_sem, warm_sem, rest_sem,
):
    core = core_ref[0]

    def block(j):
        half = jnp.where(j < HSTEPS, 1 - core, core)
        return half * HSTEPS + lax.rem(j + half * (KEPT - HSTEPS), HSTEPS)

    def column(j):
        return pl.multiple_of(block(j) * BLK, BLK)

    def spill(j):
        at = pl.ds(pl.multiple_of((block(j) - KEPT) * BLK, BLK), BLK)
        return pltpu.make_async_copy(rest_ref.at[:, at], rest_hbm.at[:, at], rest_sem.at[block(j) - KEPT])

    grads_copy = pltpu.make_async_copy(grads_hbm, grads, grads_sem)

    def copies(j):
        slot, at = lax.rem(j, SLOTS), pl.ds(column(j), BLK)
        return (
            pltpu.make_async_copy(tokens_hbm.at[:, at], tokens.at[slot], tokens_sem.at[slot]),
            pltpu.make_async_copy(memory_hbm.at[:, at], memory.at[slot], memory_sem.at[slot]),
        )

    def fetch(j):
        for copy in copies(j):
            copy.start()

    def arrive(j):
        for copy in copies(j):
            copy.wait()

    first = jnp.int32(0)
    grads_copy.start()
    fetch(first)
    warm_copy = pltpu.make_async_copy(warm_hbm, warm_copied, warm_sem)
    warm_copy.start()
    low_rows[...] = jnp.zeros_like(low_rows)
    warm[...] = jnp.zeros_like(warm)

    def on_accumulators(acc0, acc1, part0, part1):
        accs, sums = (acc0, acc1), (part0, part1)

        def multiply(j):
            slot = lax.rem(j, SLOTS)
            for k in range(TOK // MXU):
                depth = slice(k * MXU, (k + 1) * MXU)
                for h in range(2):
                    pltpu.matmul_push_rhs(tokens[slot, depth, h * MXU : (h + 1) * MXU], k % 2, h)
                left = grads[:, depth]
                for acc in accs:
                    pltpu.matmul_acc_lhs(acc, left, k % 2)

        def finish(j):
            slot = lax.rem(j, SLOTS)
            for h, acc in enumerate(accs):
                gradient = pltpu.matmul_pop(acc)
                merged = (gradient + memory[slot, :, h * MXU : (h + 1) * MXU].astype(F32)).astype(BF16)
                high_rows[h] = merged[0:MXU]
                low_rows[h, 0 : C - MXU, :] = merged[MXU:]

                @pl.when(block(j) < KEPT)
                def _():
                    kept_ref[:, pl.ds(column(j) + h * MXU, MXU)] = merged

                @pl.when(block(j) >= KEPT)
                def _():
                    rest_ref[:, pl.ds(column(j) - WIDE + h * MXU, MXU)] = merged

            @pl.when(block(j) >= KEPT)
            def _():
                spill(j).start()

        def sketch_start(j):
            for h, part in enumerate(sums):
                pltpu.matmul_push_rhs(high_rows[h], 0, h)
                pltpu.matmul_push_rhs(low_rows[h], 1, h)
                pltpu.matmul_acc_lhs(part, warm[:, 0:MXU], 0)
                pltpu.matmul_acc_lhs(part, warm[:, MXU:], 1)

        def sketch_end(j):
            at = pl.ds(pl.multiple_of(lax.rem(block(j), HSTEPS) * LANES, LANES), LANES)
            terms = [pltpu.matmul_pop(part) for part in sums]

            def put(ref):
                for q in range(N_X):
                    term = terms[q // 2][:, q % 2 * LANES : (q % 2 + 1) * LANES].astype(ref.dtype)
                    for p in range(N_Y):
                        ref[q * N_Y + p, :, at] = term[p * ROWS : (p + 1) * ROWS]

            @pl.when(j < HSTEPS)
            def _():
                put(send_ref)

            @pl.when(j >= HSTEPS)
            def _():
                put(own_ref)

        grads_copy.wait()
        fetch(first + 1)
        arrive(first)
        for j in range(2, SLOTS):
            fetch(jnp.int32(j))
        multiply(first)
        warm_copy.wait()
        warm[:, 0:C] = warm_copied[...]
        finish(first)

        def step(j, carry):
            arrive(j)

            @pl.when(j + SLOTS - 1 < STEPS)
            def _():
                fetch(j + SLOTS - 1)

            multiply(j)
            sketch_start(j - 1)
            finish(j)
            sketch_end(j - 1)
            return carry

        lax.fori_loop(1, STEPS, step, 0)
        last = jnp.int32(STEPS - 1)
        sketch_start(last)
        sketch_end(last)
        for i in range(STEPS - KEPT):
            at = pl.ds(i * BLK, BLK)
            pltpu.make_async_copy(rest_ref.at[:, at], rest_hbm.at[:, at], rest_sem.at[i]).wait()

    pl.run_scoped(
        on_accumulators,
        pltpu.ACC(0)((C, MXU), F32),
        pltpu.ACC(1)((C, MXU), F32),
        pltpu.ACC(0)((R, MXU), F32),
        pltpu.ACC(1)((R, MXU), F32),
    )


def merge(core, grads_t, tokens, memory, warm_t):
    vmem, hbm = pl.BlockSpec(memory_space=pltpu.VMEM), pl.BlockSpec(memory_space=pltpu.HBM)
    return pl.pallas_call(
        merge_body,
        out_shape=(
            jax.ShapeDtypeStruct((C, WIDE), BF16),
            jax.ShapeDtypeStruct((C, D - WIDE), BF16),
            pltpu.HBM((C, D - WIDE), BF16),
            jax.ShapeDtypeStruct((PARTS, ROWS, COLS), BF16),
            jax.ShapeDtypeStruct((PARTS, ROWS, COLS), F32),
        ),
        in_specs=[pl.BlockSpec(memory_space=pltpu.SMEM), hbm, hbm, hbm, hbm],
        out_specs=(vmem, vmem, hbm, vmem, vmem),
        scratch_shapes=[
            pltpu.VMEM((C, TOK), BF16),
            pltpu.VMEM((SLOTS, TOK, BLK), BF16),
            pltpu.VMEM((SLOTS, C, BLK), BF16),
            pltpu.VMEM((2, MXU, MXU), BF16),
            pltpu.VMEM((2, MXU, MXU), BF16),
            pltpu.VMEM((R, 2 * MXU), BF16),
            pltpu.VMEM((R, C), BF16),
            pltpu.SemaphoreType.DMA(()),
            pltpu.SemaphoreType.DMA((SLOTS,)),
            pltpu.SemaphoreType.DMA((SLOTS,)),
            pltpu.SemaphoreType.DMA(()),
            pltpu.SemaphoreType.DMA((STEPS - KEPT,)),
        ],
        compiler_params=pltpu.CompilerParams(vmem_limit_bytes=24 * MIB),
        cost_estimate=pl.CostEstimate(flops=2 * C * D * (TOK + R), bytes_accessed=30_000_000, transcendentals=0),
        name="merge",
    )(core, *(pltpu.with_memory_space_constraint(x, pltpu.HBM) for x in (grads_t, tokens, memory, warm_t)))


def half_terms(half, parts_ref, kept_ref, rest_ref, sketch_ref, total_ref):
    for b in range(HSTEPS):
        for q in range(N_X):
            at = slice(b * GROUP + q * LANES, b * GROUP + (q + 1) * LANES)
            for p in range(N_Y):
                sketch_ref[p * ROWS : (p + 1) * ROWS, at] = parts_ref[q * N_Y + p, :, b * LANES : (b + 1) * LANES]
    sketch = sketch_ref[...]
    over = WIDE - HALF

    @pl.when(half == 0)
    def _():
        total_ref[...] = lax.dot_general(sketch, kept_ref[:, :HALF], NT, preferred_element_type=F32)

    @pl.when(half == 1)
    def _():
        low = lax.dot_general(sketch[:, :over], kept_ref[:, HALF:], NT, preferred_element_type=F32)
        total_ref[...] = low + lax.dot_general(sketch[:, over:], rest_ref[...], NT, preferred_element_type=F32)

    return lax.dot_general(sketch, sketch, NT, preferred_element_type=F32)


def own_body(core_ref, parts_ref, kept_ref, rest_ref, total_ref, gram_ref, sketch_ref):
    gram_ref[...] = half_terms(core_ref[0], parts_ref, kept_ref, rest_ref, sketch_ref, total_ref)


def other_body(
    core_ref, parts_ref, kept_ref, rest_ref, own_ref, own_gram_ref, coeff_ref, gram_ref, sketch_ref, total_ref
):
    gram = half_terms(1 - core_ref[0], parts_ref, kept_ref, rest_ref, sketch_ref, total_ref)
    gram_ref[...] = gram + own_gram_ref[...]
    coeff = total_ref[...] + own_ref[...]
    each = R // N_DP
    for i in range(N_DP):
        coeff_ref[i, :, 0:C] = coeff[i * each : (i + 1) * each]
        coeff_ref[i, :, C:] = jnp.zeros((each, PAD - C), F32)


def own_terms(core, parts, kept, rest):
    vmem = pl.BlockSpec(memory_space=pltpu.VMEM)
    return pl.pallas_call(
        own_body,
        out_shape=(
            jax.ShapeDtypeStruct((R, C), F32),
            jax.ShapeDtypeStruct((R, R), F32),
            jax.ShapeDtypeStruct((R, HALF), BF16),
        ),
        in_specs=[pl.BlockSpec(memory_space=pltpu.SMEM), vmem, vmem, vmem],
        out_specs=(vmem, vmem, vmem),
        compiler_params=pltpu.CompilerParams(vmem_limit_bytes=8 * MIB),
        cost_estimate=pl.CostEstimate(flops=C * D * R, bytes_accessed=2_500_000, transcendentals=0),
        name="own_terms",
    )(core, parts, kept, rest)


def coefficients(core, parts, kept, rest, own, own_gram):
    vmem = pl.BlockSpec(memory_space=pltpu.VMEM)
    return pl.pallas_call(
        other_body,
        out_shape=(
            jax.ShapeDtypeStruct((N_DP, R // N_DP, PAD), F32),
            jax.ShapeDtypeStruct((R, R), F32),
            jax.ShapeDtypeStruct((R, HALF), BF16),
        ),
        in_specs=[pl.BlockSpec(memory_space=pltpu.SMEM), vmem, vmem, vmem, vmem, vmem],
        out_specs=(vmem, vmem, vmem),
        scratch_shapes=[pltpu.VMEM((R, C), F32)],
        compiler_params=pltpu.CompilerParams(vmem_limit_bytes=8 * MIB),
        cost_estimate=pl.CostEstimate(flops=C * D * R, bytes_accessed=2_500_000, transcendentals=0),
        name="coefficients",
    )(core, parts, kept, rest, own, own_gram)


def basis_body(core_ref, gram_ref, own_ref, other_ref, inverse_ref, basis_ref):
    row = lax.broadcasted_iota(jnp.int32, (R, R), 0)
    col = lax.broadcasted_iota(jnp.int32, (R, R), 1)
    state = jnp.concatenate([gram_ref[...], (row == col).astype(F32)], axis=1)
    index = lax.broadcasted_iota(jnp.int32, (R, 1), 0)
    spread = lambda x: jnp.broadcast_to(x, (x.shape[0], 2 * R))
    for j in range(0, R, 2):
        top = j // 8 * 8
        lead, second = state[j : j + 1, :], state[j + 1 : j + 2, :]
        corner, below, last = spread(lead[:, j + 1 : j + 2]), spread(second[:, j : j + 1]), spread(second[:, j + 1 : j + 2])
        scale = 1.0 / spread(lead[:, j : j + 1])
        lower = below * scale
        pivot = 1.0 / (last - lower * corner)
        left, right = spread(state[top:, j : j + 1]), spread(state[top:, j + 1 : j + 2])
        right = right - left * (corner * scale)
        left = jnp.where(index[top:] > j, left, 0.0)
        right = jnp.where(index[top:] > j + 1, right, 0.0)
        tail = state[top:, :] - left * (lead * scale) - right * ((second - lower * lead) * pivot)
        state = tail if top == 0 else jnp.concatenate([state[:top], tail], axis=0)
    diagonal = jnp.sum(jnp.where(row == col, state[:, :R], 0.0), axis=1, keepdims=True)
    inverse = state[:, R:] * lax.rsqrt(diagonal)
    inverse_ref[...] = inverse
    high = inverse.astype(BF16)
    rest = inverse - high.astype(F32)
    middle = rest.astype(BF16)
    low = (rest - middle.astype(F32)).astype(BF16)
    core = core_ref[0]
    for ref, half in ((own_ref, core), (other_ref, 1 - core)):
        sketch = ref[...]
        out = jnp.dot(high, sketch, preferred_element_type=F32)
        out += jnp.dot(middle, sketch, preferred_element_type=F32)
        out += jnp.dot(low, sketch, preferred_element_type=F32)
        basis_ref[:, pl.ds(pl.multiple_of(half * HALF, LANES), HALF)] = out.astype(BF16)


def basis(core, gram, own, other):
    vmem = pl.BlockSpec(memory_space=pltpu.VMEM)
    return pl.pallas_call(
        basis_body,
        out_shape=(jax.ShapeDtypeStruct((R, R), F32), jax.ShapeDtypeStruct((R, D), BF16)),
        in_specs=[pl.BlockSpec(memory_space=pltpu.SMEM), vmem, vmem, vmem],
        out_specs=(vmem, vmem),
        compiler_params=pltpu.CompilerParams(vmem_limit_bytes=8 * MIB),
        cost_estimate=pl.CostEstimate(flops=2 * R * R * D * 6, bytes_accessed=20_000_000, transcendentals=0),
        name="basis",
    )(core, gram, own, other)


def decode_body(
    total_ref, inverse_ref, basis_ref, kept_ref, rest_hbm, update_hbm, error_hbm, start_ref,
    rest, update, error, rest_sem, update_sem, error_sem,
):
    rest_copy = pltpu.make_async_copy(rest_hbm, rest, rest_sem)
    rest_copy.start()
    total = jnp.concatenate([total_ref[i, :, 0:C] for i in range(N_DP)], axis=0)
    start = jnp.dot(inverse_ref[...], total, precision=lax.Precision.HIGHEST, preferred_element_type=F32) * (1.0 / N_DP)
    start_ref[...] = start
    half = start.astype(BF16).T

    def copies(j):
        at = pl.ds(pl.multiple_of(j * DBLK, DBLK), DBLK)
        return (
            pltpu.make_async_copy(update.at[:, at], update_hbm.at[:, at], update_sem.at[j]),
            pltpu.make_async_copy(error.at[:, at], error_hbm.at[:, at], error_sem.at[j]),
        )

    def block(j, source, base):
        at = pl.ds(pl.multiple_of(j * DBLK, DBLK), DBLK)
        of = pl.ds(pl.multiple_of(j * DBLK - base, DBLK), DBLK)
        decoded = jnp.dot(half, basis_ref[:, at], preferred_element_type=F32)
        update[:, at] = decoded.astype(BF16)
        error[:, at] = (source[:, of].astype(F32) - decoded).astype(BF16)
        for copy in copies(j):
            copy.start()

    def from_kept(j, carry):
        block(j, kept_ref, 0)
        return carry

    def from_rest(j, carry):
        block(j, rest, WIDE)
        return carry

    def drain(j, carry):
        for copy in copies(j):
            copy.wait()
        return carry

    lax.fori_loop(0, WIDE // DBLK, from_kept, 0)
    rest_copy.wait()
    lax.fori_loop(WIDE // DBLK, DSTEPS, from_rest, 0)
    lax.fori_loop(0, DSTEPS, drain, 0)


DBLK = 1024
DSTEPS = D // DBLK


def decode(total, inverse, basis_t, kept, rest):
    vmem, hbm = pl.BlockSpec(memory_space=pltpu.VMEM), pl.BlockSpec(memory_space=pltpu.HBM)
    return pl.pallas_call(
        decode_body,
        out_shape=(
            jax.ShapeDtypeStruct((C, D), BF16),
            jax.ShapeDtypeStruct((C, D), BF16),
            jax.ShapeDtypeStruct((R, C), F32),
        ),
        in_specs=[vmem, vmem, vmem, vmem, hbm],
        out_specs=(hbm, hbm, vmem),
        scratch_shapes=[
            pltpu.VMEM((C, D - WIDE), BF16),
            pltpu.VMEM((C, D), BF16),
            pltpu.VMEM((C, D), BF16),
            pltpu.SemaphoreType.DMA(()),
            pltpu.SemaphoreType.DMA((DSTEPS,)),
            pltpu.SemaphoreType.DMA((DSTEPS,)),
        ],
        compiler_params=pltpu.CompilerParams(vmem_limit_bytes=16 * MIB),
        cost_estimate=pl.CostEstimate(flops=2 * C * D * R, bytes_accessed=10_500_000, transcendentals=0),
        name="decode",
    )(total, inverse, basis_t, kept, pltpu.with_memory_space_constraint(rest, pltpu.HBM))


def add_up_body(parts_ref, out_ref):
    total = jnp.sum(parts_ref[...].astype(F32), axis=0).astype(out_ref.dtype)
    for i in range(out_ref.shape[0]):
        out_ref[i] = total


def add_up(parts, copies):
    vmem = pl.BlockSpec(memory_space=pltpu.VMEM)
    return pl.pallas_call(
        add_up_body,
        out_shape=jax.ShapeDtypeStruct((copies, *parts.shape[1:]), parts.dtype),
        in_specs=[vmem],
        out_specs=vmem,
        compiler_params=pltpu.CompilerParams(vmem_limit_bytes=4 * MIB),
        cost_estimate=pl.CostEstimate(flops=parts.size, bytes_accessed=2 * parts.size, transcendentals=0),
        name="add_up",
    )(parts)


def per_device(activations, out_grads, error_memory, warm_start):
    core = lax.axis_index("core").astype(jnp.int32).reshape(1)
    swap = [(0, 1), (1, 0)]
    kept, rest, rest_hbm, send, own = merge(core, out_grads.T, activations, error_memory[0], warm_start.T)
    mine = (own + lax.ppermute(send, "core", swap).astype(F32)).astype(BF16)
    parts = lax.all_to_all(mine, ("y", "x"), 0, 0, tiled=True)
    parts = lax.all_to_all(add_up(parts, N_Z), "z", 0, 0, tiled=True)
    parts_own = lax.all_to_all(add_up(parts, PARTS), ("y", "x"), 0, 0, tiled=True)
    parts_other = lax.ppermute(parts_own, "core", swap)
    own_total, own_gram, sketch_own = own_terms(core, parts_own, kept, rest)
    coeff, gram, sketch_other = coefficients(core, parts_other, kept, rest, own_total, own_gram)
    terms = lax.all_to_all(coeff, ("y", "z"), 0, 0, tiled=True)
    total = lax.all_to_all(add_up(terms, N_DP), ("y", "z"), 0, 0, tiled=True)
    inverse, basis_t = basis(core, gram, sketch_own, sketch_other)
    update, new_error, start_t = decode(total, inverse, basis_t, kept, rest_hbm)
    return update, new_error[None], start_t.T


def solution(mesh):
    fine = Mesh(mesh.devices.reshape(N_Y, N_Z, N_X, 2), ("y", "z", "x", "core"))
    d, t = ("y", "z"), ("x", "core")
    return jax.shard_map(
        per_device,
        mesh=fine,
        in_specs=(P(d, None), P(d, t), P(d, t, None), P(t, None)),
        out_specs=(P(t, None), P(d, t, None), P(t, None)),
        check_vma=False,
    )
```
